768 devices in a mesh: rep: 12 (over z_hi, x), shard: 64 (over y, z_lo, core).
Axes of the slice: x: 4, y: 8, z: 12 (z_hi: 3, z_lo: 4; z = z_hi * 4 + z_lo), core: 2. Of those that a mesh axis runs over, the one named last changes fastest.
Arguments:
- activations: bfloat16 [1536, 12288], P('rep', 'shard'), may hold values from -6 to 6
- cotangent: bfloat16 [1536, 8192], P('rep', 'shard'), may hold values from -0.15625 to 0.15625
- weight: bfloat16 [12288, 8192], P('shard'), may hold values from -2.5 to 2.5
- master: float32 [12288, 8192], P(('shard', 'rep')), may hold values from -0.12 to 0.12
- moment: float32 [12288, 8192], P(('shard', 'rep')), may hold values from -1.2 to 1.2
- second: float32 [12288, 8192], P(('shard', 'rep')), may hold values from 0.1 to 2
- average: float32 [12288, 8192], P(('shard', 'rep')), may hold values from -0.12 to 0.12
Outputs:
- new_master: float32 [12288, 8192], P(('shard', 'rep'))
- new_moment: float32 [12288, 8192], P(('shard', 'rep'))
- new_second: float32 [12288, 8192], P(('shard', 'rep'))
- new_average: float32 [12288, 8192], P(('shard', 'rep'))
- parameters: bfloat16 [12288, 8192], P('shard')
- grad_hidden: bfloat16 [1536, 12288], P('rep', 'shard')
The draws below stay inside these ranges and needn't reach their ends.
All inputs are finite; a program needn't handle non-finite values.
Results may differ from the reference program's by a relative error of at most 0.0065.
Values may be sent and summed in bfloat16 or wider, within the bound.
A program may use at most 64 MiB of HBM per device.

```python
import math
import jax
import jax.numpy as jnp
from jax import lax

D = 8192
TOK_G = 128
STEP = 10
FF = 12288
TOKENS = 1536
N_REP = 12


def block_levels(own_key, dims, pieces, least, high):
    factor_of, own = 1.0, jax.random.fold_in(own_key, 6)
    for axis_at, blocks in pieces:
        heights = jnp.exp(jax.random.uniform(jax.random.fold_in(own, axis_at), (blocks,), jnp.float32, least / len(pieces), high / len(pieces)))
        factor_of = factor_of * jnp.repeat(heights, dims[axis_at] // blocks).reshape([-1 if axis == axis_at else 1 for axis in range(len(dims))])
    return factor_of


def normal_values(own_key, dims, deviation, most, pieces=(), dtype=jnp.bfloat16):
    result = jax.random.normal(own_key, dims, jnp.float32) * deviation
    if len(pieces) > 0:
        result = block_levels(own_key, dims, pieces, -0.22, 0.18) * result
    return jnp.clip(result, min=-most, max=most).astype(dtype)


def setup_inputs(seed: int = 0) -> dict:
    seeds = jax.random.split(jax.random.key(seed), 8)
    activations = normal_values(seeds[0], (TOKENS, FF), 1.0, 6.0, ((0, 12), (1, 64)))
    cotangent = normal_values(seeds[1], (TOKENS, D), TOKENS ** -0.5, 0.15625, ((0, 12), (1, 64)))
    weight = normal_values(seeds[2], (FF, D), (max(D // TOKENS, 1)) ** -0.5, 2.5, ((0, 64),))
    master = normal_values(seeds[3], (FF, D), 0.02, 0.12, ((0, 768),), jnp.float32)
    moment = normal_values(seeds[4], (FF, D), 0.2, 1.2, ((0, 768),), jnp.float32)
    second = jnp.clip(jnp.exp(math.log(2.0) - 2.9957323 * jax.random.uniform(seeds[5], (FF, D), jnp.float32) ** block_levels(seeds[5], (FF, D), ((0, 768),), -0.2, 0.2)), 0.1, 2.0)
    average = normal_values(seeds[6], (FF, D), 0.02, 0.12, ((0, 768),), jnp.float32)
    return {"activations": activations, "cotangent": cotangent, "weight": weight, "master": master, "moment": moment, "second": second, "average": average}


def reference(activations, cotangent, weight, master, moment, second, average):
    gradient = jnp.zeros((activations.shape[1], cotangent.shape[1]), jnp.float32)
    for replica in range(N_REP):
        rows_act = activations[replica * TOK_G:(replica + 1) * TOK_G]
        rows_cot = cotangent[replica * TOK_G:(replica + 1) * TOK_G]
        partial_sum = jnp.dot(rows_act.T, rows_cot, preferred_element_type=jnp.float32)
        rounded = lax.optimization_barrier(partial_sum.astype(jnp.bfloat16))
        gradient = gradient + rounded.astype(jnp.float32)
    grad_hidden = jnp.dot(cotangent, weight.T, preferred_element_type=jnp.float32).astype(jnp.bfloat16)
    first_fix = 1.0 - 0.9 ** STEP
    second_fix = 1.0 - 0.999 ** STEP
    ema_decay = min(0.999, (1.0 + STEP) / (10.0 + STEP))
    new_moment = 0.9 * moment + 0.1 * gradient
    new_second = 0.999 * second + 0.001 * gradient * gradient
    update = new_moment / first_fix / (jnp.sqrt(new_second / second_fix) + 1e-08) + 0.1 * master
    new_master = master - 0.01 * update
    new_average = ema_decay * average + (1.0 - ema_decay) * new_master
    parameters = new_master.astype(jnp.bfloat16)
    return (new_master, new_moment, new_second, new_average, parameters, grad_hidden)
```

```python
import jax
import jax.numpy as jnp
from jax import lax
from jax.experimental import pallas as pl
from jax.experimental.pallas import tpu as pltpu
from jax.sharding import PartitionSpec as P

STEP = 10
MESH = pl.DeviceIdType.MESH
F32, BF16 = jnp.float32, jnp.bfloat16
NX, NY, NZ, NH, NL = 4, 8, 12, 3, 4
TOK, FB = 128, 128
K = NH * TOK
UNITS, UC = 16, 512
YT = 14
LAG_C, LAG_D, LAG_E, LAG_G = 2, 4, 6, 8


def chip(x, y, z, c):
    return ((z // NL) * NX + x, (y * NL + z % NL) * 2 + c)


def unit_place(u):
    j = jnp.maximum(u - 2, 0)
    s = j // 4 + 1
    slot = jnp.where(u < 2, 0, jnp.where(j % 2 == 0, s, NY - s))
    pair = jnp.where(u < 2, u, jnp.where(u == UNITS - 1, 1, (j // 2) % 2))
    return slot, pair


def kernel(
    act_t, cot, weight, master, moment, second, average,
    o_master, o_moment, o_second, o_average, o_params, o_hidden,
    feats, at_v, lhs_all, lhs, wv, st, part, got, own, par, acc,
    in_sem, a_s, a_r, f_s, f_r, b_s, b_r, yp_s, yp_r, ym_s, ym_r, c_s, c_r,
    r_s, r_r, z_s, z_r, x_s, x_r, w_s, w_r,
):
    rep, shard = lax.axis_index("rep"), lax.axis_index("shard")
    zh, x = rep // NX, rep % NX
    y, zl, c = shard // 8, (shard // 2) % NL, shard % 2
    z = zh * NL + zl

    def at(dx=0, dy=0, dz=0):
        return chip((x + dx) % NX, (y + dy) % NY, (z + dz) % NZ, c)

    partner = chip(x, y, z, 1 - c)
    far = 2 + 8 * c
    far_back = 10 - 8 * c
    turn = 1 + 2 * c

    def send(src, dst, ssem, rsem, to):
        return pltpu.make_async_remote_copy(
            src_ref=src, dst_ref=dst, send_sem=ssem, recv_sem=rsem, device_id=to, device_id_type=MESH
        )

    loads = [
        pltpu.make_async_copy(cot, feats.at[0, c, 0, pl.ds(zh * TOK, TOK)], in_sem.at[0]),
        pltpu.make_async_copy(act_t, at_v, in_sem.at[1]),
        pltpu.make_async_copy(weight, wv, in_sem.at[2]),
    ] + [
        pltpu.make_async_copy(ref, st.at[n], in_sem.at[3 + n])
        for n, ref in enumerate((master, moment, second, average))
    ]
    for load in loads:
        load.start()

    barrier = pltpu.get_barrier_semaphore()
    sources = [at(dz=4), at(dz=8), at(dz=1), at(dz=11), at(dz=far_back), at(dy=1), at(dy=7), at(dx=1), at(dx=2), at(dx=3), partner]
    for source in sources:
        pl.semaphore_signal(barrier, inc=1, device_id=source, device_id_type=MESH)
    pl.semaphore_wait(barrier, len(sources))

    loads[0].wait()
    mine = feats.at[0, c, 0, pl.ds(zh * TOK, TOK)]
    for d in (1, 2):
        send(mine, mine, f_s.at[d - 1], f_r.at[d - 1], at(dz=4 * d)).start()
    loads[1].wait()
    lhs_all[zh] = at_v[pl.ds(pl.multiple_of(zh * 64, 64), 64), :]

    def act_copy(d):
        rows = pl.ds(pl.multiple_of(((zh + d) % NH) * 64, 64), 64)
        return send(at_v.at[rows], lhs_all.at[zh], a_s.at[d - 1], a_r.at[d - 1], at(dz=4 * d))

    for d in (1, 2):
        act_copy(d).start()
    for d in (1, 2):
        send(mine, mine, f_s.at[d - 1], f_r.at[d - 1], at(dz=4 * d)).wait_recv()

    first = feats.at[0, c, 0]

    def bundle(n):
        to = (1, 11, far)[n]
        return send(first, feats.at[0, c, (2, 1, 3)[n]], b_s.at[n], b_r.at[n], at(dz=to))

    for n in range(3):
        bundle(n).start()

    def y_plus(s, i, j):
        return send(feats.at[s, c, i], feats.at[s + 1, c, i], yp_s.at[j], yp_r.at[j], at(dy=1))

    def y_minus(s, i, j):
        return send(
            feats.at[(NY - s) % NY, c, i], feats.at[NY - s - 1, c, i], ym_s.at[j], ym_r.at[j], at(dy=7)
        )

    def across(u):
        slot, pair = unit_place(u)
        ref = feats.at[slot, c, pl.ds(pair * 2, 2)]
        return send(ref, ref, c_s.at[u], c_r.at[u], partner)

    for i in range(4):
        if i:
            bundle((1, 0, 2)[i - 1]).wait_recv()
        y_plus(0, i, i).start()
        y_minus(0, i, i).start()
        if i % 2:
            across(i // 2).start()

    for d in (1, 2):
        act_copy(d).wait_recv()
    for d in range(NX):
        rows = pl.ds(pl.multiple_of(((x + d) % NX) * 16, 16), 16)
        for h in range(NH):
            lhs[d * 16 : (d + 1) * 16, h * TOK : (h + 1) * TOK] = lhs_all[h, rows, :]
    acc[...] = jnp.zeros_like(acc)
    for load in loads[2:]:
        load.wait()

    def columns(u, k):
        slot, pair = unit_place(u)
        i = pair * 2 + k
        low = (zl + jnp.where(i == 2, 3, jnp.where(i == 3, 2, i))) % NL
        return pl.ds(pl.multiple_of(((y - slot + NY) % NY) * 1024 + low * 256, 256), 256)

    def reduce_copy(u, d):
        return send(part.at[u, d - 1], got.at[u, d - 1], r_s.at[u, d - 1], r_r.at[u, d - 1], at(dx=d))

    def z_copy(u, d):
        return send(par.at[u, 0, 0], par.at[u, 0, NH - d], z_s.at[u, d - 1], z_r.at[u, d - 1], at(dz=4 * d))

    def x_copy(u, n):
        return send(par.at[u, 0], par.at[u, 3 - 2 * n], x_s.at[u, n], x_r.at[u, n], at(dx=1 + 2 * n))

    def w_copy(u):
        return send(par.at[u, 3 - 2 * c], par.at[u, 2], w_s.at[u], w_r.at[u], at(dx=turn))

    first_fix = 1.0 - 0.9**STEP
    second_fix = 1.0 - 0.999**STEP
    decay = min(0.999, (1.0 + STEP) / (10.0 + STEP))

    def pass_on(j):
        s, i = j // 4 + 1, j % 4
        i_minus = i + jnp.where(j >= 12, 2, 0)
        y_plus(s - 1, i, j).wait_recv()

        @pl.when(j < 10)
        def _():
            y_plus(s, i, j + 4).start()

        y_minus(s - 1, i_minus, j).wait_recv()

        @pl.when((j < 8) | ((j >= 10) & (j < 12)))
        def _():
            y_minus(s, i_minus, jnp.where(j < 8, j + 4, j + 2)).start()

        @pl.when(j % 2 == 1)
        def _():
            across(j + 1).start()
            across(j + 2).start()

    def multiply(u):
        slot, pair = unit_place(u)
        across(u).wait_recv()
        for k in (0, 1):
            i = pair * 2 + k
            right = jnp.concatenate([feats[slot, 0, i], feats[slot, 1, i]], axis=1)
            grad = jnp.dot(lhs[...], right, preferred_element_type=F32)
            own[u, :, k * 256 : (k + 1) * 256] = grad[:16]
            for d in range(1, NX):
                part[u, d - 1, :, k * 256 : (k + 1) * 256] = grad[d * 16 : (d + 1) * 16].astype(BF16)
        for d in (2, 1, 3):
            reduce_copy(u, d).start()
        for k in (0, 1):
            i = pair * 2 + k
            rows = pl.ds(pl.multiple_of(zh * TOK, TOK), TOK)
            left = jnp.concatenate([feats[slot, 0, i, rows, :], feats[slot, 1, i, rows, :]], axis=1)
            acc[...] += lax.dot_general(
                wv[:, columns(u, k)], left, (((1,), (1,)), ((), ())), preferred_element_type=F32
            )

    def update(u):
        for d in (1, 2, 3):
            reduce_copy(u, d).wait_recv()
        for k in (0, 1):
            here, cols = slice(k * 256, (k + 1) * 256), columns(u, k)
            gradient = own[u, :, here]
            for d in (1, 2, 3):
                gradient = gradient + got[u, d - 1, :, here].astype(F32)
            new_moment = 0.9 * st[1, :, cols] + 0.1 * gradient
            new_second = 0.999 * st[2, :, cols] + 0.001 * gradient * gradient
            old = st[0, :, cols]
            step = new_moment / first_fix / (jnp.sqrt(new_second / second_fix) + 1e-08) + 0.1 * old
            new_master = old - 0.01 * step
            par[u, 0, 0, :, here] = new_master.astype(BF16)
            o_master[:, cols] = new_master
            o_moment[:, cols] = new_moment
            o_second[:, cols] = new_second
            o_average[:, cols] = decay * st[3, :, cols] + (1.0 - decay) * new_master
        for d in (1, 2):
            z_copy(u, d).start()

    def spread_x(u):
        for d in (1, 2):
            z_copy(u, d).wait_recv()
        for n in (0, 1):
            x_copy(u, n).start()

    def spread_far(u):
        x_copy(u, c).wait_recv()
        w_copy(u).start()

    def finish(u):
        x_copy(u, 1 - c).wait_recv()
        w_copy(u).wait_recv()
        for a in range(NX):
            for b in range(NH):
                rows = pl.ds(pl.multiple_of((((zh + b) % NH) * NX + (x + a) % NX) * 16, 16), 16)
                for k in (0, 1):
                    o_params[rows, columns(u, k)] = par[u, a, b, :, k * 256 : (k + 1) * 256]
        across(u).wait_send()
        for d in (1, 2, 3):
            reduce_copy(u, d).wait_send()
        for d in (1, 2):
            z_copy(u, d).wait_send()
        for n in (0, 1):
            x_copy(u, n).wait_send()
        w_copy(u).wait_send()

        @pl.when(u < YT)
        def _():
            y_plus(0, 0, u).wait_send()
            y_minus(0, 0, u).wait_send()

    def tick(t, _):
        def stage(f, lag, count=UNITS):
            u = t - lag

            @pl.when((u >= 0) & (u < count))
            def _():
                f(u)

        stage(pass_on, 0, YT)
        stage(spread_far, LAG_E)
        stage(spread_x, LAG_D)
        stage(update, LAG_C)
        stage(multiply, 0)
        stage(finish, LAG_G)
        return 0

    lax.fori_loop(0, UNITS + LAG_G, tick, 0)
    o_hidden[...] = acc[...].astype(BF16)
    for d in (1, 2):
        send(mine, mine, f_s.at[d - 1], f_r.at[d - 1], at(dz=4 * d)).wait_send()
        act_copy(d).wait_send()
    for n in range(3):
        bundle(n).wait_send()


def shards(activations, cotangent, weight, master, moment, second, average):
    rows, width = master.shape
    hidden = weight.shape[0]
    dma = pltpu.SemaphoreType.DMA
    vmem = pltpu.VMEM
    operands = (activations.T, cotangent, weight, master, moment, second, average)
    operands = [pltpu.with_memory_space_constraint(a, pltpu.HBM) for a in operands]
    *updated, hidden_grad = pl.pallas_call(
        kernel,
        out_shape=[vmem((rows, width), F32)] * 4 + [vmem((hidden, width), BF16), vmem((hidden, TOK), BF16)],
        in_specs=[pl.BlockSpec(memory_space=pltpu.HBM)] * 7,
        out_specs=[pl.BlockSpec(memory_space=pltpu.VMEM)] * 6,
        scratch_shapes=[
            vmem((NY, 2, NL, K, FB), BF16),
            vmem((hidden, TOK), BF16),
            vmem((NH, hidden // NH, TOK), BF16),
            vmem((hidden // NH, K), BF16),
            vmem((hidden, width), BF16),
            vmem((4, rows, width), F32),
            vmem((UNITS, 3, 16, UC), BF16),
            vmem((UNITS, 3, 16, UC), BF16),
            vmem((UNITS, 16, UC), F32),
            vmem((UNITS, NX, NH, 16, UC), BF16),
            vmem((hidden, TOK), F32),
            dma((7,)),
            dma((2,)), dma((2,)), dma((2,)), dma((2,)), dma((3,)), dma((3,)),
            dma((YT,)), dma((YT,)), dma((YT,)), dma((YT,)), dma((UNITS,)), dma((UNITS,)),
            dma((UNITS, 3)), dma((UNITS, 3)), dma((UNITS, 2)), dma((UNITS, 2)),
            dma((UNITS, 2)), dma((UNITS, 2)), dma((UNITS,)), dma((UNITS,)),
        ],
        compiler_params=pltpu.CompilerParams(
            collective_id=0, has_side_effects=True, vmem_limit_bytes=22 * 1024 * 1024
        ),
    )(*operands)
    return *updated, hidden_grad.T


def solution(mesh):
    row = P(("shard", "rep"), None)
    both = P("rep", "shard")
    wide = P("shard", None)
    return jax.shard_map(
        shards,
        mesh=mesh,
        in_specs=(both, both, wide, row, row, row, row),
        out_specs=(row, row, row, row, wide, both),
        check_vma=False,
    )
```

```python
import jax
import jax.numpy as jnp
from jax import lax
from jax.experimental import pallas as pl
from jax.experimental.pallas import tpu as pltpu
from jax.sharding import PartitionSpec as P

STEP = 10
MESH = pl.DeviceIdType.MESH
F32, BF16 = jnp.float32, jnp.bfloat16
NX, NY, NZ, NH, NL = 4, 8, 12, 3, 4
TOK, FB = 128, 128
K = NH * TOK
UNITS, UC = 16, 512
YT = 14
LAG_C, LAG_D, LAG_E, LAG_G = 2, 5, 8, 10
LAG_H = 4


def chip(x, y, z, c):
    return ((z // NL) * NX + x, (y * NL + z % NL) * 2 + c)


ORDER = (
    (0, 0), (0, 1), (1, 0), (7, 0), (1, 1), (7, 1), (2, 0), (6, 0),
    (2, 1), (6, 1), (3, 0), (5, 0), (3, 1), (5, 1), (4, 0), (4, 1),
)
STEPS = (
    (0, 2, 4, 4, 6, 6, 8, 8, 10, 10, 12, 12, 14, 14, 14, 14),
    (0, 0, 0, 2, 4, 4, 6, 6, 8, 8, 10, 10, 12, 12, 14, 14),
)


def pick(table, n):
    value = table[0]
    for k in range(1, len(table)):
        if table[k] != table[k - 1]:
            value = jnp.where(n >= k, table[k], value)
    return value


def unit_place(n):
    return pick([slot for slot, _ in ORDER], n), pick([core for _, core in ORDER], n)


def kernel(
    act_t, cot, weight, master, moment, second, average,
    o_master, o_moment, o_second, o_average, o_params, o_hidden,
    feats, at_v, lhs_all, lhs, wv, st, part, got, own, par, acc,
    in_sem, a_s, a_r, f_s, f_r, b_s, b_r, yp_s, yp_r, ym_s, ym_r, c_s, c_r,
    r_s, r_r, z_s, z_r, x_s, x_r, w_s, w_r, there,
):
    rep, shard = lax.axis_index("rep"), lax.axis_index("shard")
    zh, x = rep // NX, rep % NX
    y, zl, c = shard // 8, (shard // 2) % NL, shard % 2
    z = zh * NL + zl

    def at(dx=0, dy=0, dz=0):
        return chip((x + dx) % NX, (y + dy) % NY, (z + dz) % NZ, c)

    partner = chip(x, y, z, 1 - c)
    far, far_back = at(dz=2 + 8 * c), at(dz=10 - 8 * c)
    turn = at(dx=1 + 2 * c)
    x_at = [None] + [at(dx=n) for n in (1, 2, 3)]
    y_up, y_down = at(dy=1), at(dy=7)
    z_at = [None, at(dz=4), at(dz=8)]
    z_up, z_down = at(dz=1), at(dz=11)

    def send(src, dst, ssem, rsem, to):
        return pltpu.make_async_remote_copy(
            src_ref=src, dst_ref=dst, send_sem=ssem, recv_sem=rsem, device_id=to, device_id_type=MESH
        )

    loads = [
        pltpu.make_async_copy(cot, feats.at[0, c, 0, pl.ds(zh * TOK, TOK)], in_sem.at[0]),
        pltpu.make_async_copy(act_t, at_v, in_sem.at[1]),
        pltpu.make_async_copy(weight, wv, in_sem.at[2]),
    ] + [
        pltpu.make_async_copy(ref, st.at[n], in_sem.at[3 + n])
        for n, ref in enumerate((master, moment, second, average))
    ]
    for load in loads:
        load.start()

    barrier = pltpu.get_barrier_semaphore()
    sources = [*z_at[1:], z_up, z_down, far_back, y_up, y_down, *x_at[1:]]
    for source in sources:
        pl.semaphore_signal(barrier, inc=1, device_id=source, device_id_type=MESH)

    @pl.when(c == 0)
    def _():
        pl.semaphore_signal(barrier, inc=1, device_id=partner, device_id_type=MESH)

    pl.semaphore_wait(barrier, len(sources) + c)

    @pl.when(c == 1)
    def _():
        pl.semaphore_signal(there, inc=1, device_id=partner, device_id_type=MESH)

    loads[0].wait()
    mine = feats.at[0, c, 0, pl.ds(zh * TOK, TOK)]
    for d in (1, 2):
        send(mine, mine, f_s.at[d - 1], f_r.at[d - 1], z_at[d]).start()
    loads[1].wait()
    lhs_all[zh] = at_v[pl.ds(pl.multiple_of(zh * 64, 64), 64), :]

    def act_copy(d):
        rows = pl.ds(pl.multiple_of(((zh + d) % NH) * 64, 64), 64)
        return send(at_v.at[rows], lhs_all.at[zh], a_s.at[d - 1], a_r.at[d - 1], z_at[d])

    for d in (1, 2):
        act_copy(d).start()
    for d in (1, 2):
        send(mine, mine, f_s.at[d - 1], f_r.at[d - 1], z_at[d]).wait_recv()

    first = feats.at[0, c, 0]

    def bundle(n):
        return send(first, feats.at[0, c, (2, 1, 3)[n]], b_s.at[n], b_r.at[n], (z_up, z_down, far)[n])

    for n in range(3):
        bundle(n).start()

    def y_plus(s, i, j):
        return send(feats.at[s, c, i], feats.at[s + 1, c, i], yp_s.at[j], yp_r.at[j], y_up)

    def y_minus(s, i, j):
        return send(
            feats.at[(NY - s) % NY, c, i], feats.at[NY - s - 1, c, i], ym_s.at[j], ym_r.at[j], y_down
        )

    def across(slot):
        ref = feats.at[slot, c]
        return send(ref, ref, c_s.at[slot], c_r.at[slot], partner)

    def across_here(slot):
        ref = feats.at[slot, 1 - c]
        return send(ref, ref, c_s.at[slot], c_r.at[slot], partner)

    for i in range(4):
        if i:
            bundle((1, 0, 2)[i - 1]).wait_recv()
        y_plus(0, i, i).start()
        y_minus(0, i, i).start()

    @pl.when(c == 0)
    def _():
        pl.semaphore_wait(there, 1)

    across(0).start()

    for d in (1, 2):
        act_copy(d).wait_recv()
    for d in range(NX):
        rows = pl.ds(pl.multiple_of(((x + d) % NX) * 16, 16), 16)
        for h in range(NH):
            lhs[d * 16 : (d + 1) * 16, h * TOK : (h + 1) * TOK] = lhs_all[h, rows, :]
    acc[...] = jnp.zeros_like(acc)
    for load in loads[2:]:
        load.wait()

    def columns(u):
        slot, core = unit_place(u)
        low = ((y - slot + NY) % NY) * 1024 + core * 128
        return [pl.ds(pl.multiple_of(low + ((zl + r) % NL) * 256, 128), 128) for r in (0, 1, 3, 2)]

    def reduce_copy(u, d):
        return send(part.at[u, d - 1], got.at[u, d - 1], r_s.at[u, d - 1], r_r.at[u, d - 1], x_at[d])

    def z_copy(u, d):
        return send(par.at[u, 0, 0], par.at[u, 0, NH - d], z_s.at[u, d - 1], z_r.at[u, d - 1], z_at[d])

    def x_copy(u, n):
        return send(par.at[u, 0], par.at[u, 3 - 2 * n], x_s.at[u, n], x_r.at[u, n], x_at[1 + 2 * n] if isinstance(n, int) else turn)

    def w_copy(u):
        return send(par.at[u, 3 - 2 * c], par.at[u, 2], w_s.at[u], w_r.at[u], turn)

    first_fix = 1.0 - 0.9**STEP
    second_fix = 1.0 - 0.999**STEP
    decay = min(0.999, (1.0 + STEP) / (10.0 + STEP))

    def pass_on(j):
        s, i = j // 4 + 1, j % 4
        i_minus = i + jnp.where(j >= 12, 2, 0)
        y_plus(s - 1, i, j).wait_recv()

        @pl.when(j < 10)
        def _():
            y_plus(s, i, j + 4).start()

        y_minus(s - 1, i_minus, j).wait_recv()

        @pl.when((j < 8) | ((j >= 10) & (j < 12)))
        def _():
            y_minus(s, i_minus, jnp.where(j < 8, j + 4, j + 2)).start()

        @pl.when((j % 4 == 3) & (j < 12))
        def _():
            across(s).start()
            across(NY - s).start()

        @pl.when(j == YT - 1)
        def _():
            across(NY // 2).start()

    def multiply(u):
        slot, core = unit_place(u)

        @pl.when(core != c)
        def _():
            across_here(slot).wait_recv()

        for k in (0, 1):
            right = jnp.concatenate([feats[slot, core, 2 * k], feats[slot, core, 2 * k + 1]], axis=1)
            grad = jnp.dot(lhs[...], right, preferred_element_type=F32)
            own[u, :, k * 256 : (k + 1) * 256] = grad[:16]
            for d in range(1, NX):
                part[u, d - 1, :, k * 256 : (k + 1) * 256] = grad[d * 16 : (d + 1) * 16].astype(BF16)
        for d in (2, 1, 3):
            reduce_copy(u, d).start()

    def multiply_hidden(u):
        slot, core = unit_place(u)
        rows = pl.ds(pl.multiple_of(zh * TOK, TOK), TOK)
        left = jnp.concatenate([feats[slot, core, i, rows, :] for i in range(4)], axis=1)
        right = jnp.concatenate([wv[:, run] for run in columns(u)], axis=1)
        acc[...] += lax.dot_general(right, left, (((1,), (1,)), ((), ())), preferred_element_type=F32)

    def update(u):
        for d in (1, 2, 3):
            reduce_copy(u, d).wait_recv()
        for i, cols in enumerate(columns(u)):
            here = slice(i * 128, (i + 1) * 128)
            gradient = own[u, :, here]
            for d in (1, 2, 3):
                gradient = gradient + got[u, d - 1, :, here].astype(F32)
            new_moment = 0.9 * st[1, :, cols] + 0.1 * gradient
            new_second = 0.999 * st[2, :, cols] + 0.001 * gradient * gradient
            old = st[0, :, cols]
            step = new_moment / first_fix / (jnp.sqrt(new_second / second_fix) + 1e-08) + 0.1 * old
            new_master = old - 0.01 * step
            par[u, 0, 0, :, here] = new_master.astype(BF16)
            o_master[:, cols] = new_master
            o_moment[:, cols] = new_moment
            o_second[:, cols] = new_second
            o_average[:, cols] = decay * st[3, :, cols] + (1.0 - decay) * new_master
        for d in (1, 2):
            z_copy(u, d).start()

    def spread_x(u):
        for d in (1, 2):
            z_copy(u, d).wait_recv()
        for n in (0, 1):
            x_copy(u, n).start()

    def spread_far(u):
        x_copy(u, c).wait_recv()
        w_copy(u).start()

    def finish(u):
        x_copy(u, 1 - c).wait_recv()
        w_copy(u).wait_recv()
        for a in range(NX):
            for b in range(NH):
                rows = pl.ds(pl.multiple_of((((zh + b) % NH) * NX + (x + a) % NX) * 16, 16), 16)
                for i, cols in enumerate(columns(u)):
                    o_params[rows, cols] = par[u, a, b, :, i * 128 : (i + 1) * 128]
        for d in (1, 2, 3):
            reduce_copy(u, d).wait_send()
        for d in (1, 2):
            z_copy(u, d).wait_send()
        for n in (0, 1):
            x_copy(u, n).wait_send()
        w_copy(u).wait_send()

        @pl.when(u < YT)
        def _():
            y_plus(0, 0, u).wait_send()
            y_minus(0, 0, u).wait_send()

    def tick(t, done):
        def stage(f, lag, count=UNITS):
            u = t - lag

            @pl.when((u >= 0) & (u < count))
            def _():
                f(u)

        steps = jnp.where(c == 0, pick(STEPS[0], t), pick(STEPS[1], t))
        lax.fori_loop(done, steps, lambda j, _: pass_on(j), None)
        stage(spread_far, LAG_E)
        stage(spread_x, LAG_D)
        stage(update, LAG_C)
        stage(multiply, 0)
        stage(multiply_hidden, LAG_H)
        stage(finish, LAG_G)
        return steps

    lax.fori_loop(0, UNITS + LAG_G, tick, 0)
    o_hidden[...] = acc[...].astype(BF16)
    for d in (1, 2):
        send(mine, mine, f_s.at[d - 1], f_r.at[d - 1], z_at[d]).wait_send()
        act_copy(d).wait_send()
    for n in range(3):
        bundle(n).wait_send()
    for slot in range(NY):
        across(slot).wait_send()


def write(*refs):
    half = (len(refs) - 1) // 2
    copies = [pltpu.make_async_copy(refs[n], refs[half + n], refs[-1].at[n]) for n in range(half)]
    for copy in copies:
        copy.start()
    for copy in copies:
        copy.wait()


def shards(activations, cotangent, weight, master, moment, second, average):
    rows, width = master.shape
    hidden = weight.shape[0]
    dma = pltpu.SemaphoreType.DMA
    vmem = pltpu.VMEM
    operands = (activations.T, cotangent, weight, master, moment, second, average)
    operands = [pltpu.with_memory_space_constraint(a, pltpu.HBM) for a in operands]
    results = pl.pallas_call(
        kernel,
        out_shape=[vmem((rows, width), F32)] * 4 + [vmem((hidden, width), BF16), vmem((hidden, TOK), BF16)],
        in_specs=[pl.BlockSpec(memory_space=pltpu.HBM)] * 7,
        out_specs=[pl.BlockSpec(memory_space=pltpu.VMEM)] * 6,
        scratch_shapes=[
            vmem((NY, 2, NL, K, FB), BF16),
            vmem((hidden, TOK), BF16),
            vmem((NH, hidden // NH, TOK), BF16),
            vmem((hidden // NH, K), BF16),
            vmem((hidden, width), BF16),
            vmem((4, rows, width), F32),
            vmem((UNITS, 3, 16, UC), BF16),
            vmem((UNITS, 3, 16, UC), BF16),
            vmem((UNITS, 16, UC), F32),
            vmem((UNITS, NX, NH, 16, UC), BF16),
            vmem((hidden, TOK), F32),
            dma((7,)),
            dma((2,)), dma((2,)), dma((2,)), dma((2,)), dma((3,)), dma((3,)),
            dma((YT,)), dma((YT,)), dma((YT,)), dma((YT,)), dma((NY,)), dma((NY,)),
            dma((UNITS, 3)), dma((UNITS, 3)), dma((UNITS, 2)), dma((UNITS, 2)),
            dma((UNITS, 2)), dma((UNITS, 2)), dma((UNITS,)), dma((UNITS,)),
            pltpu.SemaphoreType.REGULAR,
        ],
        compiler_params=pltpu.CompilerParams(
            collective_id=0, has_side_effects=True, vmem_limit_bytes=22 * 1024 * 1024
        ),
    )(*operands)
    shapes = [jax.ShapeDtypeStruct(r.shape, r.dtype) for r in results]
    *updated, hidden_grad = pl.pallas_call(
        write,
        out_shape=shapes,
        in_specs=[pl.BlockSpec(memory_space=pltpu.VMEM)] * 6,
        out_specs=[pl.BlockSpec(memory_space=pl.ANY)] * 6,
        scratch_shapes=[dma((6,))],
        compiler_params=pltpu.CompilerParams(vmem_limit_bytes=1024 * 1024),
    )(*[pltpu.with_memory_space_constraint(r, pltpu.VMEM) for r in results])
    return *updated, hidden_grad.T


def solution(mesh):
    row = P(("shard", "rep"), None)
    both = P("rep", "shard")
    wide = P("shard", None)
    return jax.shard_map(
        shards,
        mesh=mesh,
        in_specs=(both, both, wide, row, row, row, row),
        out_specs=(row, row, row, row, wide, both),
        check_vma=False,
    )
```
